128 devices in a mesh: cuts: 8 (over z, y_hi), frame: 16 (over x, y_lo, core).
Axes of the slice: x: 4, y: 4 (y_hi: 2, y_lo: 2; y = y_hi * 2 + y_lo), z: 4, core: 2. Of those that a mesh axis runs over, the one named last changes fastest.
Arguments:
- cine_image: float32 [8, 16, 192, 384], P('cuts', 'frame'), may hold values from -6 to 6
- coil_maps: bfloat16 [8, 12, 192, 384], P('cuts'), may hold values from -4 to 4
- caipi_shift: int32 [8], P('cuts'), may hold values from 0 to 3
- line_mask: int32 [16, 192], P('frame'), may hold values 0 or 1
- measured: bfloat16 [8, 16, 12, 48, 384], P('cuts', 'frame'), may hold values from -6 to 6
- spatial_weight: float32 [32, 2, 3, 3], replicated, may hold values from -1.5 to 1.5
- temporal_weight: float32 [3, 32, 32], replicated, may hold values from -0.625 to 0.625
- project_weight: float32 [2, 32], replicated, may hold values from -1 to 1
Outputs:
- refined: float32 [8, 16, 192, 384], P('cuts', 'frame')
The draws below stay inside these ranges and needn't reach their ends.
Inputs may be any that keep to these rules, and one draw needn't show every extreme that they name: `line_mask`: 1 where a line of a frame is sampled, else 0.
All inputs are finite; a program needn't handle non-finite values. No bound on the sum of `line_mask` on one device may be relied on, other than what follows from the above.
Results may differ from the reference program's by a relative error of at most 0.0023.
Values may be sent and summed in bfloat16 or wider, within the bound.
No kernel may reach another device: no remote copies, remote signals or barrier semaphores. Data moves between devices by JAX's collectives and lax.ppermute only.
A program may use at most 320 MiB of HBM per device.

```python
import math
import jax
import jax.numpy as jnp
from jax import lax

H = 192
W = 192
COILS = 12
CH = 32
MB = 4
SLICES = 8
FRAMES = 16
SPACING = 2
QROWS = 48


def place_ends(entries, own_key, low, top_value):
    index_at = [jax.random.randint(jax.random.fold_in(own_key, axis), (), 0, length) for axis, length in enumerate(entries.shape)]
    widest = entries.shape.index(max(entries.shape))
    beside = index_at[:widest] + [(index_at[widest] + 1) % entries.shape[widest]] + index_at[widest + 1:]
    return entries.at[tuple(index_at)].set(low).at[tuple(beside)].set(top_value)


def block_levels(stream_key, extent, split, least, high):
    factor_of = 1.0
    for axis_at, shards_of in split:
        heights = jax.random.uniform(jax.random.fold_in(jax.random.fold_in(stream_key, 6), axis_at), (shards_of,), jnp.float32, least / len(split), high / len(split))
        factor_of = factor_of * jnp.repeat(jnp.exp(heights), extent[axis_at] // shards_of).reshape((-1,) + (1,) * (len(extent) - 1 - axis_at))
    return factor_of


def normal_values(key, extent, scale, reach, split=(), kind=jnp.bfloat16):
    array = jax.random.normal(key, extent, jnp.float32) * scale
    if len(split) > 0:
        array = block_levels(key, extent, split, -0.22, 0.18) * array
    return jnp.clip(array, min=-reach, max=reach).astype(kind)


def setup_inputs(seed: int = 0) -> dict:
    key_of = jax.random.split(jax.random.key(seed), 9)
    return {
        "cine_image": normal_values(key_of[0], (SLICES, FRAMES, H, 2 * W), 1.0, 6.0, ((0, 8), (1, 16)), jnp.float32),
        "coil_maps": normal_values(key_of[1], (SLICES, COILS, H, 2 * W), 0.29, 4.0, ((0, 8),)),
        "caipi_shift": place_ends(jax.random.randint(key_of[2], (SLICES,), 0, MB), jax.random.fold_in(key_of[2], 1), 0, MB - 1).astype(jnp.int32),
        "line_mask": place_ends((jax.random.randint(key_of[3], (FRAMES, H), 0, 2) < 1).astype(jnp.int32), jax.random.fold_in(key_of[3], 1), 0, 1),
        "measured": normal_values(key_of[4], (SLICES, FRAMES, COILS, QROWS, 2 * W), 0.5, 6.0, ((0, 8), (1, 16))),
        "spatial_weight": normal_values(key_of[5], (CH, 2, 3, 3), 18 ** -0.5, 1.5, (), jnp.float32),
        "temporal_weight": normal_values(key_of[6], (3, CH, CH), (3 * CH) ** -0.5, 0.625, (), jnp.float32),
        "project_weight": normal_values(key_of[7], (2, CH), CH ** -0.5, 1.0, (), jnp.float32),
    }


step_rate = 0.5
exact_mode = lax.Precision.HIGHEST

def dft_tables(length):
    positions = jnp.arange(length, dtype=jnp.int32)
    phase_turns = positions[:, None] * positions[None, :] % length
    angles = phase_turns.astype(jnp.float32) * (2.0 * math.pi / length)
    factor = 1.0 / math.sqrt(length)
    return (jnp.cos(angles) * factor, jnp.sin(angles) * factor)

def row_matrix(cosine, sine_table, inverse):
    if inverse:
        upper_rows = jnp.concatenate([cosine, sine_table], 1)
        lower_rows = jnp.concatenate([-sine_table, cosine], 1)
    else:
        upper_rows = jnp.concatenate([cosine, -sine_table], 1)
        lower_rows = jnp.concatenate([sine_table, cosine], 1)
    return jnp.concatenate([upper_rows, lower_rows], 0)

def transform(source, tables_h, matrix_w, inverse):
    cos_h, sin_h = tables_h
    columns = source.shape[-1] // 2
    along_width = jnp.einsum('...hv,vu->...hu', source, matrix_w, precision=exact_mode)
    cosine_part = jnp.einsum('kh,...hu->...ku', cos_h, along_width, precision=exact_mode)
    sine_part = jnp.einsum('kh,...hu->...ku', sin_h, along_width, precision=exact_mode)
    if inverse:
        turned = jnp.concatenate([-sine_part[..., columns:], sine_part[..., :columns]], -1)
    else:
        turned = jnp.concatenate([sine_part[..., columns:], -sine_part[..., :columns]], -1)
    return cosine_part + turned

def multiply(source, factor, conjugate):
    columns = source.shape[-1] // 2
    left_re = source[..., :columns]
    left_im = source[..., columns:]
    right_re = factor[..., :columns]
    right_im = factor[..., columns:]
    if conjugate:
        real_part = left_re * right_re + left_im * right_im
        imag_part = left_im * right_re - left_re * right_im
    else:
        real_part = left_re * right_re - left_im * right_im
        imag_part = left_re * right_im + left_im * right_re
    return jnp.concatenate([real_part, imag_part], -1)

def rotate(source, phase_re, phase_im, conjugate):
    columns = source.shape[-1] // 2
    left_re = source[..., :columns]
    left_im = source[..., columns:]
    if conjugate:
        real_part = left_re * phase_re + left_im * phase_im
        imag_part = left_im * phase_re - left_re * phase_im
    else:
        real_part = left_re * phase_re - left_im * phase_im
        imag_part = left_re * phase_im + left_im * phase_re
    return jnp.concatenate([real_part, imag_part], -1)

def spatial(source, weight):
    height = source.shape[-2]
    columns = source.shape[-1] // 2
    parted = source.reshape(source.shape[:-1] + (2, columns))
    padded = jnp.pad(parted, ((0, 0), (0, 0), (1, 1), (0, 0), (1, 1)))
    summed = None
    for row_shift in range(3):
        for col_shift in range(3):
            window = padded[:, :, row_shift:row_shift + height, :, col_shift:col_shift + columns]
            partial_sum = jnp.einsum('oc,sfhcw->sfohw', weight[:, :, row_shift, col_shift], window, precision=exact_mode)
            summed = partial_sum if summed is None else summed + partial_sum
    return summed

def reference(cine_image, coil_maps, caipi_shift, line_mask, measured, spatial_weight, temporal_weight, project_weight):
    tables_h = dft_tables(H)
    cos_w, sine_w = dft_tables(W)
    forward_w = row_matrix(cos_w, sine_w, False)
    inverse_w = row_matrix(cos_w, sine_w, True)
    ky_lines = jnp.arange(H, dtype=jnp.int32)
    phase_turns = caipi_shift[:, None] * ky_lines[None, :] % MB
    angles = phase_turns.astype(jnp.float32) * (2.0 * math.pi / MB)
    phase_re = jnp.cos(angles)[:, None, :, None]
    phase_im = jnp.sin(angles)[:, None, :, None]
    maps_full = coil_maps.astype(jnp.float32)
    targets = measured.astype(jnp.float32).reshape(MB, SPACING, FRAMES, COILS, QROWS, 2 * W)
    targets = jnp.transpose(targets, (2, 1, 3, 0, 4, 5)).reshape(FRAMES, SPACING, COILS, H, 2 * W)

    def one_frame(inputs):
        frame_image, mask_row, target = inputs
        coil_images = multiply(frame_image[:, None], maps_full, False)
        spectra = transform(coil_images, tables_h, forward_w, False)
        phased = rotate(spectra, phase_re, phase_im, False)
        slice_terms = phased.reshape(MB, SPACING, COILS, H, 2 * W)
        collapsed = lax.optimization_barrier(jnp.sum(slice_terms, axis=0))
        sampled = mask_row.astype(jnp.float32)[None, None, :, None]
        residual = lax.optimization_barrier((sampled * (collapsed - target)).astype(jnp.bfloat16)).astype(jnp.float32)
        spread = jnp.tile(residual, (MB, 1, 1, 1))
        turned = rotate(spread, phase_re, phase_im, True)
        coil_back = transform(turned, tables_h, inverse_w, True)
        gradient = lax.optimization_barrier(jnp.sum(multiply(coil_back, maps_full, True), axis=1))
        return frame_image - step_rate * gradient
    updated = lax.map(one_frame, (jnp.moveaxis(cine_image, 1, 0), line_mask, targets))
    updated = jnp.moveaxis(updated, 0, 1)

    def refine(slab_image):
        features = spatial(slab_image[None], spatial_weight)[0]
        prior_frame = jnp.roll(features, 1, axis=0)
        later_frame = jnp.roll(features, -1, axis=0)
        mixture = jnp.einsum('oi,fihw->fohw', temporal_weight[0], prior_frame, precision=exact_mode)
        mixture = mixture + jnp.einsum('oi,fihw->fohw', temporal_weight[1], features, precision=exact_mode)
        mixture = mixture + jnp.einsum('oi,fihw->fohw', temporal_weight[2], later_frame, precision=exact_mode)
        active = jax.nn.relu(mixture)
        project = jnp.einsum('oc,fchw->fhow', project_weight, active, precision=exact_mode)
        return slab_image + project.reshape(slab_image.shape)
    return lax.map(refine, updated)
```

```python
import math

import jax
import jax.numpy as jnp
import ml_dtypes
import numpy as np
from jax import lax
from jax.experimental import pallas as pl
from jax.experimental.pallas import tpu as pltpu
from jax.sharding import PartitionSpec as P


MB = 4
G = 4
PEERS = MB * G
SIDE = 192
COILS = 12
PER = COILS // MB
QR = SIDE // MB
SLAB = SIDE // PEERS
CHUNK = 8 * SLAB
MARK = 1e30
F32 = jnp.float32
BF16 = jnp.bfloat16
VMEM = pl.BlockSpec(memory_space=pltpu.VMEM)
SMEM = pl.BlockSpec(memory_space=pltpu.SMEM)
ANY = pl.BlockSpec(memory_space=pl.ANY)


def hi_lo(table):
    high = table.astype(ml_dtypes.bfloat16)
    low = (table - high.astype(np.float64)).astype(ml_dtypes.bfloat16)
    return high, low


def tables():
    at = np.arange(SIDE)
    angle = (at[:, None] * at[None, :] % SIDE) * (2.0 * math.pi / SIDE)
    cos = np.cos(angle) / math.sqrt(SIDE)
    sin = np.sin(angle) / math.sqrt(SIDE)
    return cos, sin


def width_matrix():
    cos, sin = tables()
    both = np.concatenate([np.concatenate([cos, -sin], 1), np.concatenate([sin, cos], 1)], 0)
    high, low = hi_lo(both)
    return np.concatenate([high, low], 0)


def folded(re, im):
    return np.concatenate([re[:, :128], re[:, 128:], im[:, 128:], im[:, :128]], 1)


def height_matrix():
    cos, sin = tables()
    real = folded(cos, sin)
    imag = folded(-sin, cos)
    both = np.concatenate([real, real, imag, imag], 0)
    return np.stack(hi_lo(both))


def line_index():
    lane = np.arange(2 * SIDE)
    line = np.where(lane < SIDE, lane, np.where(lane < 256, lane - 64, lane - 256))
    return line


def fold(re, im):
    return jnp.concatenate([re[:, :128], re[:, 128:], im[:, 128:], im[:, :128]], 1)


def dot_nt(a, b):
    return lax.dot_general(a, b, (((1,), (1,)), ((), ())), preferred_element_type=F32)


def dot_nn(a, b):
    return lax.dot_general(a, b, (((1,), (0,)), ((), ())), preferred_element_type=F32)


def pack_kernel(
    place_ref, x_ref, maps_ref, meas_ref, mask_ref, line_ref, w_ref, out_ref, maps_v, parts, stage, sem
):
    turn = place_ref[0]
    quarter = place_ref[1]
    member = place_ref[2]
    copy = pltpu.make_async_copy(maps_ref.at[pl.ds(member * PER, PER)], maps_v, sem)
    copy.start()

    def start(block):
        return pl.multiple_of(lax.rem(turn + block, MB) * QR, 16)

    lines = lax.broadcasted_iota(jnp.int32, (SIDE, 2 * SIDE), 0)
    select = (lines == line_ref[...] + quarter * QR).astype(F32).astype(BF16)
    mask8 = jnp.broadcast_to(mask_ref[...].astype(F32), (8, SIDE)).astype(BF16)
    sampled = dot_nn(mask8, select)[0:1] > 0.5
    for r in range(PER):
        rows = [
            meas_ref[PER * lax.rem(p + MB - quarter, MB) + r] for p in range(MB)
        ]
        both = dot_nt(w_ref[...], jnp.concatenate(rows, 0))
        re = both[0:SIDE] + both[2 * SIDE : 3 * SIDE]
        im = both[SIDE : 2 * SIDE] + both[3 * SIDE :]
        parts[4 + r] = jnp.where(sampled, fold(re, im), MARK)
    flipped = jnp.concatenate([x_ref[pl.ds(start(b), QR), :] for b in range(MB)], 0).T
    image = fold(flipped[:SIDE], flipped[SIDE:])
    high = image.astype(BF16).astype(F32)
    parts[3] = high
    parts[7] = image - high
    copy.wait()
    for r in range(PER):
        flipped = jnp.concatenate(
            [maps_v[r, pl.ds(start(b), QR), :] for b in range(MB)], 0
        ).astype(F32).T
        parts[r] = fold(flipped[:SIDE], flipped[SIDE:])
    for i in range(PEERS):
        for p in range(8):
            stage[i, SLAB * p : SLAB * (p + 1), :] = parts[p, SLAB * i : SLAB * (i + 1), :]
        out_ref[i] = stage[i].astype(BF16)


def slab_kernel(got_ref, a_ref, out_ref, xt, zs, ys):
    lane = lax.broadcasted_iota(jnp.int32, (40, 128), 1)
    left = lane < 64
    place = lax.broadcasted_iota(jnp.int32, (40, 2 * SIDE), 1)
    place = jnp.where(place < SIDE, place, jnp.where(place < 256, place - 64, place - 256))
    for i in range(PEERS):
        top = got_ref[i, 0:48, :].astype(F32)
        low = got_ref[i, 48:96, :].astype(F32)
        x = top[36:48] + low[36:48]
        x = jnp.concatenate([x, x, x, x[:4]], 0)
        mid = x[:, 128:256]
        turned = pltpu.roll(mid, 64, 1)
        xt[i, :, 0:128] = x[:, 0:128]
        xt[i, :, 128:256] = jnp.where(left, mid, turned)
        xt[i, :, 256:384] = jnp.where(left, -turned, mid)
        xt[i, :, 384:512] = x[:, 256:384]
    for j in range(MB):
        acc = [None] * G
        for m in range(MB):
            c = got_ref[m * G + j, 0:48, :].astype(F32)[0:40]
            c0, c1, c2 = c[:, 0:128], c[:, 128:256], c[:, 256:384]
            c1t = pltpu.roll(c1, 64, 1)
            for f in range(G):
                i = m * G + f
                x0, xa, xb, x2 = (xt[i, :, 128 * n : 128 * (n + 1)] for n in range(4))
                o0 = c0 * x0 - c2 * x2
                o1 = c1 * xa + c1t * xb
                o2 = c0 * x2 + c2 * x0
                if m > 0:
                    o0 += zs[40 * f : 40 * f + 40, 0:128]
                    o1 += zs[40 * f : 40 * f + 40, 128:256]
                    o2 += zs[40 * f : 40 * f + 40, 256:384]
                zs[40 * f : 40 * f + 40, 0:128] = o0
                zs[40 * f : 40 * f + 40, 128:256] = o1
                zs[40 * f : 40 * f + 40, 256:384] = o2
        off = QR * ((MB - j) % MB)
        pieces = ((off, 128), (off + 128, 64), (2 * SIDE + off + 128, 64), (2 * SIDE + off, 128))
        a_hi = jnp.concatenate([a_ref[0, s : s + n, :] for s, n in pieces], 0)
        a_lo = jnp.concatenate([a_ref[1, s : s + n, :] for s, n in pieces], 0)
        z = zs[...]
        zh = z.astype(BF16)
        zl = (z - zh.astype(F32)).astype(BF16)
        rows = 40 * G
        both = dot_nt(jnp.concatenate([zh, zl], 0), a_hi)
        zk = both[:rows] + both[rows:] + dot_nt(zh, a_lo)
        rest = []
        for f in range(G):
            t = None
            for p in range(MB):
                q = (p - j) % MB
                src = got_ref[q * G + f, 48:96, :].astype(F32)[0:40]
                t = src if t is None else jnp.where(place >= p * QR, src, t)
            rest.append(jnp.where(t > 0.1 * MARK, 0.0, zk[40 * f : 40 * f + 40] - t))
        r = jnp.concatenate(rest, 0)
        rh = r.astype(BF16)
        rl = (r - rh.astype(F32)).astype(BF16)
        both = dot_nn(jnp.concatenate([rh, rl], 0), a_hi)
        ys[j] = both[:rows] + both[rows:] + dot_nn(rh, a_lo)
    for m in range(MB):
        acc = [None] * G
        for j in range(MB):
            c = got_ref[m * G + j, 0:48, :].astype(F32)[0:40]
            c0, c1, c2 = c[:, 0:128], c[:, 128:256], c[:, 256:384]
            c1t = pltpu.roll(c1, 64, 1)
            ca = jnp.where(left, c1, c1t)
            cb = jnp.where(left, c1t, -c1)
            for f in range(G):
                y = ys[j, 40 * f : 40 * f + 40, :]
                y0, y1, y2 = y[:, 0:128], y[:, 128:256], y[:, 256:384]
                o = jnp.concatenate(
                    [c0 * y0 + c2 * y2, ca * y1 + cb * pltpu.roll(y1, 64, 1), c0 * y2 - c2 * y0], 1
                )
                acc[f] = o if acc[f] is None else acc[f] + o
        for f in range(G):
            total = acc[f][0:12] + acc[f][12:24] + acc[f][24:36]
            high = total.astype(BF16).astype(F32)
            out_ref[m * G + f] = jnp.concatenate([high, total - high], 0).astype(BF16)


def update_kernel(place_ref, x_ref, back_ref, out_ref, turned, grad):
    turn = place_ref[0]
    for i in range(PEERS):
        both = back_ref[i].astype(F32)
        turned[SLAB * i : SLAB * (i + 1), :] = both[:SLAB] + both[SLAB:]
    re = turned[:, 0:SIDE]
    im = jnp.concatenate([turned[:, 256:384], turned[:, 192:256]], 1)
    grad[...] = jnp.concatenate([re, im], 0).T
    for b in range(MB):
        at = pl.multiple_of(lax.rem(b + MB - turn, MB) * QR, 16)
        rows = slice(b * QR, (b + 1) * QR)
        out_ref[rows, :] = x_ref[rows, :] - 0.5 * grad[pl.ds(at, QR), :]


def refine_kernel(prior_ref, own_ref, later_ref, m_ref, p_ref, out_ref, lay):
    zeros = jnp.zeros((18, 8, SIDE), F32)
    lay[:, 0:8, :] = zeros
    lay[:, 192:200, :] = zeros
    column = lax.broadcasted_iota(jnp.int32, (SIDE, SIDE), 1)
    for t, ref in enumerate((prior_ref, own_ref, later_ref)):
        u = ref[...]
        for p in range(2):
            for b in range(3):
                by = (1 - b - SIDE * p) % (2 * SIDE)
                v = (pltpu.roll(u, by, 1) if by else u)[:, :SIDE]
                if b == 0:
                    v = jnp.where(column == 0, 0.0, v)
                if b == 2:
                    v = jnp.where(column == SIDE - 1, 0.0, v)
                lay[(t * 2 + p) * 3 + b, 1 : SIDE + 1, :] = v

    def step(i, carry):
        at = pl.multiple_of(i * 8, 8)
        window = lay[:, pl.ds(at, 16), :].reshape(18 * 16, SIDE)
        high = window.astype(BF16)
        low = (window - high.astype(F32)).astype(BF16)
        mix = dot_nn(m_ref[...], jnp.concatenate([high, low, high], 0))
        re = None
        im = None
        for o in range(32):
            v = jnp.maximum(mix[8 * o : 8 * o + 8], 0.0)
            re = v * p_ref[0, o] if re is None else re + v * p_ref[0, o]
            im = v * p_ref[1, o] if im is None else im + v * p_ref[1, o]
        out_ref[pl.ds(at, 8), :] = own_ref[pl.ds(at, 8), :] + jnp.concatenate([re, im], 1)
        return carry

    lax.fori_loop(0, SIDE // 8, step, 0)


def params(mib):
    return pltpu.CompilerParams(vmem_limit_bytes=mib * 1024 * 1024)


def groups(cuts, frames):
    found = {}
    for c in range(cuts):
        for f in range(frames):
            found.setdefault((c % (cuts // MB), f // G), []).append(c * frames + f)
    return list(found.values())


def mixing_matrix(spatial_weight, temporal_weight):
    joint = jnp.einsum(
        "toi,ipab->otpab", temporal_weight, spatial_weight, precision=lax.Precision.HIGHEST
    )
    gap = np.arange(16)[None, :] - np.arange(8)[:, None]
    matrix = 0.0
    for a in range(3):
        hit = jnp.asarray((gap == a).astype(np.float32))
        matrix = matrix + joint[:, None, :, :, a, :, None] * hit[None, :, None, None, None, :]
    matrix = matrix.reshape(256, 18 * 16)
    high = matrix.astype(BF16)
    low = (matrix - high.astype(F32)).astype(BF16)
    return jnp.concatenate([high, high, low], 1)


def on_device(
    cine_image,
    coil_maps,
    caipi_shift,
    line_mask,
    measured,
    spatial_weight,
    temporal_weight,
    project_weight,
):
    cuts = lax.axis_size("cuts")
    frames = lax.axis_size("frame")
    quarter = lax.axis_index("cuts") // (cuts // MB)
    member = lax.axis_index("frame") % G
    place = jnp.stack([caipi_shift[0], quarter, member]).astype(jnp.int32)
    image = cine_image[0, 0]
    send = pl.pallas_call(
        pack_kernel,
        out_shape=jax.ShapeDtypeStruct((PEERS, CHUNK, 2 * SIDE), BF16),
        in_specs=[SMEM, VMEM, ANY, VMEM, VMEM, VMEM, VMEM],
        out_specs=VMEM,
        scratch_shapes=[
            pltpu.VMEM((PER, SIDE, 2 * SIDE), BF16),
            pltpu.VMEM((8, SIDE, 2 * SIDE), F32),
            pltpu.VMEM((PEERS, CHUNK, 2 * SIDE), F32),
            pltpu.SemaphoreType.DMA,
        ],
        compiler_params=params(32),
        name="pack",
    )(
        place,
        image,
        coil_maps[0],
        measured[0, 0],
        line_mask,
        jnp.asarray((line_index() % QR).astype(np.int32))[None],
        jnp.asarray(width_matrix()),
    )
    where = groups(cuts, frames)
    got = lax.all_to_all(send, ("cuts", "frame"), 0, 0, axis_index_groups=where)
    slab = pl.pallas_call(
        slab_kernel,
        out_shape=jax.ShapeDtypeStruct((PEERS, 2 * SLAB, 2 * SIDE), BF16),
        in_specs=[VMEM, VMEM],
        out_specs=VMEM,
        scratch_shapes=[
            pltpu.VMEM((PEERS, 40, 512), F32),
            pltpu.VMEM((40 * G, 2 * SIDE), F32),
            pltpu.VMEM((MB, 40 * G, 2 * SIDE), F32),
        ],
        compiler_params=params(32),
        name="slab",
    )(got, jnp.asarray(height_matrix()))
    back = lax.all_to_all(slab, ("cuts", "frame"), 0, 0, axis_index_groups=where)
    updated = pl.pallas_call(
        update_kernel,
        out_shape=jax.ShapeDtypeStruct((SIDE, 2 * SIDE), F32),
        in_specs=[SMEM, VMEM, VMEM],
        out_specs=VMEM,
        scratch_shapes=[pltpu.VMEM((SIDE, 2 * SIDE), F32), pltpu.VMEM((SIDE, 2 * SIDE), F32)],
        compiler_params=params(16),
        name="update",
    )(place, image, back)
    forward = [(i, (i + 1) % frames) for i in range(frames)]
    prior = lax.ppermute(updated, "frame", forward)
    later = lax.ppermute(updated, "frame", [(b, a) for a, b in forward])
    refined = pl.pallas_call(
        refine_kernel,
        out_shape=jax.ShapeDtypeStruct((SIDE, 2 * SIDE), F32),
        in_specs=[VMEM, VMEM, VMEM, VMEM, SMEM],
        out_specs=VMEM,
        scratch_shapes=[pltpu.VMEM((18, 208, SIDE), F32)],
        compiler_params=params(32),
        name="refine",
    )(prior, updated, later, mixing_matrix(spatial_weight, temporal_weight), project_weight)
    return refined[None, None]


def solution(mesh):
    return jax.shard_map(
        on_device,
        mesh=mesh,
        in_specs=(
            P("cuts", "frame", None, None),
            P("cuts", None, None, None),
            P("cuts"),
            P("frame", None),
            P("cuts", "frame", None, None, None),
            P(),
            P(),
            P(),
        ),
        out_specs=P("cuts", "frame", None, None),
        check_vma=False,
    )
```

```python
import math

import jax
import jax.numpy as jnp
import ml_dtypes
import numpy as np
from jax import lax
from jax.experimental import pallas as pl
from jax.experimental.pallas import tpu as pltpu
from jax.sharding import PartitionSpec as P


MB = 4
G = 4
PEERS = MB * G
SIDE = 192
COILS = 12
PER = COILS // MB
QR = SIDE // MB
SLAB = SIDE // PEERS
CHUNK = 8 * SLAB
MARK = 1e30
F32 = jnp.float32
BF16 = jnp.bfloat16
VMEM = pl.BlockSpec(memory_space=pltpu.VMEM)
SMEM = pl.BlockSpec(memory_space=pltpu.SMEM)
ANY = pl.BlockSpec(memory_space=pl.ANY)
HBM = pl.BlockSpec(memory_space=pltpu.HBM)


def hi_lo(table):
    high = table.astype(ml_dtypes.bfloat16)
    low = (table - high.astype(np.float64)).astype(ml_dtypes.bfloat16)
    return high, low


def tables():
    at = np.arange(SIDE)
    angle = (at[:, None] * at[None, :] % SIDE) * (2.0 * math.pi / SIDE)
    cos = np.cos(angle) / math.sqrt(SIDE)
    sin = np.sin(angle) / math.sqrt(SIDE)
    return cos, sin


def width_matrix():
    cos, sin = tables()
    both = np.concatenate([np.concatenate([cos, -sin], 1), np.concatenate([sin, cos], 1)], 0)
    high, low = hi_lo(both)
    return np.concatenate([high, low], 0)


def folded(re, im):
    return np.concatenate([re[:, :128], re[:, 128:], im[:, 128:], im[:, :128]], 1)


def height_matrix():
    cos, sin = tables()
    real = folded(cos, sin)
    imag = folded(-sin, cos)
    both = np.concatenate([real, real, imag, imag], 0)
    return np.stack(hi_lo(both))


def line_pieces(group):
    off = QR * ((MB - group) % MB)
    return ((off, 128), (off + 128, 64), (2 * SIDE + off + 128, 64), (2 * SIDE + off, 128))


def slab_matrices():
    table = height_matrix()
    turned = []
    for j in range(MB):
        rows = np.concatenate([table[:, s : s + n] for s, n in line_pieces(j)], 1)
        turned.append(np.swapaxes(rows, 1, 2))
    return np.stack(turned + [table[:, : 2 * SIDE], table[:, 2 * SIDE :]])


def fold(re, im):
    return jnp.concatenate([re[:, :128], re[:, 128:], im[:, 128:], im[:, :128]], 1)


def dot_nt(a, b):
    return lax.dot_general(a, b, (((1,), (1,)), ((), ())), preferred_element_type=F32)


def dot_nn(a, b):
    return lax.dot_general(a, b, (((1,), (0,)), ((), ())), preferred_element_type=F32)


def pack_kernel(
    turn_ref, x_hbm, maps_hbm, meas_hbm, mask_hbm, w_hbm, out_hbm,
    x_ref, maps_ref, meas_ref, mask_ref, w_ref, parts, out_ref, sems, out_sems,
):
    turn = turn_ref[0]
    quarter = lax.axis_index("cuts") // (lax.axis_size("cuts") // MB)
    member = lax.rem(lax.axis_index("frame"), G)
    loads = [
        pltpu.make_async_copy(src, dst, sems.at[n])
        for n, (src, dst) in enumerate(
            (
                (x_hbm, x_ref),
                (maps_hbm.at[pl.ds(member * PER, PER)], maps_ref),
                (mask_hbm, mask_ref),
                (w_hbm, w_ref),
                (meas_hbm, meas_ref),
            )
        )
    ]
    for load in loads:
        load.start()

    def start(block):
        return pl.multiple_of(lax.rem(turn + block, MB) * QR, 16)

    loads[0].wait()
    flipped = jnp.concatenate([x_ref[pl.ds(start(b), QR), :] for b in range(MB)], 0).T
    image = fold(flipped[:SIDE], flipped[SIDE:])
    high = image.astype(BF16).astype(F32)
    parts[3] = high
    parts[7] = image - high
    loads[1].wait()
    for r in range(PER):
        flipped = jnp.concatenate(
            [maps_ref[r, pl.ds(start(b), QR), :] for b in range(MB)], 0
        ).astype(F32).T
        parts[r] = fold(flipped[:SIDE], flipped[SIDE:])
    lane = lax.broadcasted_iota(jnp.int32, (SIDE, 2 * SIDE), 1)
    line = jnp.where(lane < SIDE, lane, jnp.where(lane < 256, lane - 64, lane - 256))
    for _ in range(MB - 1):
        line = jnp.where(line >= QR, line - QR, line)
    lines = lax.broadcasted_iota(jnp.int32, (SIDE, 2 * SIDE), 0)
    select = (lines == line + quarter * QR).astype(F32).astype(BF16)
    loads[2].wait()
    mask8 = jnp.broadcast_to(mask_ref[...].astype(F32), (8, SIDE)).astype(BF16)
    sampled = dot_nn(mask8, select)[0:1] > 0.5
    loads[3].wait()
    loads[4].wait()
    for r in range(PER):
        rows = [meas_ref[PER * lax.rem(p + MB - quarter, MB) + r] for p in range(MB)]
        both = dot_nt(w_ref[...], jnp.concatenate(rows, 0))
        re = both[0:SIDE] + both[2 * SIDE : 3 * SIDE]
        im = both[SIDE : 2 * SIDE] + both[3 * SIDE :]
        parts[4 + r] = jnp.where(sampled, fold(re, im), MARK)
    for i in range(PEERS):
        tiles = [parts[p, 8 * i : 8 * i + 8, :] for p in range(8)]
        out_ref[i, 0:64, :] = jnp.concatenate(tiles, 0).astype(BF16)
        tiles = [parts[p, 128 + 4 * i : 132 + 4 * i, :] for p in range(8)]
        out_ref[i, 64:96, :] = jnp.concatenate(tiles, 0).astype(BF16)
        pltpu.make_async_copy(out_ref.at[i], out_hbm.at[i], out_sems.at[i]).start()
    for i in range(PEERS):
        pltpu.make_async_copy(out_ref.at[i], out_hbm.at[i], out_sems.at[i]).wait()


def cut(value):
    return [value[8 * t : 8 * t + 8] for t in range(value.shape[0] // 8)]


def slab_kernel(got_ref, a_ref, out_hbm, xs, cs, zs, ys, out_ref, sems):
    left = lax.broadcasted_iota(jnp.int32, (8, 128), 1) < 64
    lane = lax.broadcasted_iota(jnp.int32, (8, 128), 1)
    low16 = (lane < 16) | ((lane >= 64) & (lane < 80))
    for i in range(PEERS):
        main = got_ref[i, 0:32, :].astype(F32)
        half = got_ref[i, 64:80, :].astype(F32)
        x8 = main[24:32] + got_ref[i, 32:64, :].astype(F32)[24:32]
        x4 = (half[8:16] + got_ref[i, 80:96, :].astype(F32)[8:16])[4:8]
        for t, x in enumerate((x8, jnp.concatenate([x4, x4], 0))):
            mid = x[:, 128:256]
            turned = pltpu.roll(mid, 64, 1)
            xs[i, t, :, 0:128] = x[:, 0:128]
            xs[i, t, :, 128:256] = jnp.where(left, mid, turned)
            xs[i, t, :, 256:384] = jnp.where(left, -turned, mid)
            xs[i, t, :, 384:512] = x[:, 256:384]
        for t, c in enumerate(cut(main[0:24]) + cut(half)):
            cs[i, t, :, 0:384] = c
            cs[i, t, :, 384:512] = pltpu.roll(c[:, 128:256], 64, 1)

    def gather(j):
        for t in range(5):
            acc = [None] * G
            for m in range(MB):
                c0, c1, c2, c1t = (cs[m * G + j, t, :, 128 * n : 128 * n + 128] for n in range(4))
                for f in range(G):
                    x0, xa, xb, x2 = (
                        xs[m * G + f, t // 3, :, 128 * n : 128 * n + 128] for n in range(4)
                    )
                    o = (c0 * x0 - c2 * x2, c1 * xa + c1t * xb, c0 * x2 + c2 * x0)
                    acc[f] = o if m == 0 else tuple(p + q for p, q in zip(acc[f], o))
            for f in range(G):
                for n in range(3):
                    zs[j, 40 * f + 8 * t : 40 * f + 8 * t + 8, 128 * n : 128 * n + 128] = acc[f][n]

    def matrices(j):
        return [
            jnp.concatenate(
                [
                    a_ref[MB + s // (2 * SIDE), h, s % (2 * SIDE) : s % (2 * SIDE) + n, :]
                    for s, n in line_pieces(j)
                ],
                0,
            )
            for h in range(2)
        ]

    def triple(value, high, low):
        top = value.astype(BF16)
        rest = (value - top.astype(F32)).astype(BF16)
        return dot_nn(
            jnp.concatenate([top, rest, top], 1), jnp.concatenate([high, high, low], 0)
        )

    def residual(j, zk):
        out = []
        for f in range(G):
            sources = []
            for p in range(MB):
                i = ((p - j) % MB) * G + f
                main = got_ref[i, 32:64, :].astype(F32)[0:24]
                sources.append(cut(main) + cut(got_ref[i, 80:96, :].astype(F32)))
            for t in range(5):
                row = 40 * f + 8 * t
                s0, s1, s2, s3 = (source[t] for source in sources)
                outer = [
                    jnp.where(lane < 48, s0[:, n], jnp.where(lane < 96, s1[:, n], s2[:, n]))
                    for n in (slice(0, 128), slice(256, 384))
                ]
                mid = jnp.where(low16, s2[:, 128:256], s3[:, 128:256])
                target = jnp.concatenate([outer[0], mid, outer[1]], 1)
                out.append(jnp.where(target > 0.1 * MARK, 0.0, zk[row : row + 8] - target))
        return jnp.concatenate(out, 0)

    gather(0)
    for j in range(MB):
        zk = triple(zs[j], a_ref[j, 0], a_ref[j, 1])
        if j + 1 < MB:
            gather(j + 1)
        y = triple(residual(j, zk), *matrices(j))
        ys[j, :, 0:384] = y
        ys[j, :, 384:512] = pltpu.roll(y[:, 128:256], 64, 1)

    for m in range(MB):
        sums = []
        for tiles in ((0, 1, 2), (3,), (4,)):
            acc = [None] * G
            for t in tiles:
                for j in range(MB):
                    c0, c1, c2, c1t = (
                        cs[m * G + j, t, :, 128 * n : 128 * n + 128] for n in range(4)
                    )
                    ca = jnp.where(left, c1, c1t)
                    cb = jnp.where(left, c1t, -c1)
                    for f in range(G):
                        row = 40 * f + 8 * t
                        y0, y1, y2, y1t = (
                            ys[j, row : row + 8, 128 * n : 128 * n + 128] for n in range(4)
                        )
                        o = (c0 * y0 + c2 * y2, ca * y1 + cb * y1t, c0 * y2 - c2 * y0)
                        acc[f] = o if acc[f] is None else tuple(p + q for p, q in zip(acc[f], o))
            sums.append([jnp.concatenate(o, 1) for o in acc])
        for f in range(G):
            i = m * G + f
            main, third, fourth = (part[f] for part in sums)
            half = third[0:4] + third[4:8] + fourth[0:4]
            main_hi = main.astype(BF16).astype(F32)
            half_hi = half.astype(BF16).astype(F32)
            out_ref[i] = jnp.concatenate(
                [main_hi, main - main_hi, half_hi, half - half_hi], 0
            ).astype(BF16)
            pltpu.make_async_copy(out_ref.at[i], out_hbm.at[i], sems.at[i]).start()
    for i in range(PEERS):
        pltpu.make_async_copy(out_ref.at[i], out_hbm.at[i], sems.at[i]).wait()


def update_kernel(turn_ref, x_ref, back_ref, out_ref, edge_ref, turned, grad):
    turn = turn_ref[0]
    for i in range(PEERS):
        both = back_ref[i].astype(F32)
        turned[8 * i : 8 * i + 8, :] = both[0:8] + both[8:16]
        turned[128 + 4 * i : 132 + 4 * i, :] = both[16:20] + both[20:24]
    re = turned[:, 0:SIDE]
    im = jnp.concatenate([turned[:, 256:384], turned[:, 192:256]], 1)
    grad[...] = jnp.concatenate([re, im], 0).T
    for b in range(MB):
        at = pl.multiple_of(lax.rem(b + MB - turn, MB) * QR, 16)
        rows = slice(b * QR, (b + 1) * QR)
        u = x_ref[rows, :] - 0.5 * grad[pl.ds(at, QR), :]
        out_ref[rows, :] = u
        edge_ref[rows, :] = u.astype(BF16)


def spread(lay, frames):
    zeros = jnp.zeros((lay.shape[0], 8, SIDE), F32)
    lay[:, 0:8, :] = zeros
    lay[:, 192:200, :] = zeros
    column = lax.broadcasted_iota(jnp.int32, (SIDE, SIDE), 1)
    for t, u in enumerate(frames):
        for p in range(2):
            for b in range(3):
                by = (1 - b - SIDE * p) % (2 * SIDE)
                v = (pltpu.roll(u, by, 1) if by else u)[:, :SIDE]
                if b == 0:
                    v = jnp.where(column == 0, 0.0, v)
                if b == 2:
                    v = jnp.where(column == SIDE - 1, 0.0, v)
                lay[(t * 2 + p) * 3 + b, 1 : SIDE + 1, :] = v


def dot_exact(a, b):
    return lax.dot_general(
        a, b, (((1,), (0,)), ((), ())), precision=lax.Precision.HIGHEST, preferred_element_type=F32
    )


def mixing_matrices(temporal_ref, spatial_ref):
    odd = lax.rem(lax.axis_index("frame"), 2) == 1
    before, after = temporal_ref[0], temporal_ref[2]
    joint = [
        dot_exact(side, spatial_ref[...])
        for side in (
            jnp.where(odd, before, after),
            temporal_ref[1],
            jnp.where(odd, after, before),
        )
    ]

    def build(blocks):
        width = 96 * len(blocks)
        lane = lax.broadcasted_iota(jnp.int32, (18, width), 1)
        entry = lax.broadcasted_iota(jnp.int32, (18, width), 0)
        block = sum((lane >= 96 * n).astype(jnp.int32) for n in range(1, len(blocks)))
        channel = (lane - 96 * block) >> 4
        part = (channel >= 3).astype(jnp.int32)
        at = lax.broadcasted_iota(jnp.int32, (256, width), 1)
        gap = (at & 15) - (lax.broadcasted_iota(jnp.int32, (256, width), 0) & 7)
        total = jnp.zeros((256, width), F32)
        for a in range(3):
            table = (entry == part * 6 + a * 3 + channel).astype(F32)
            picked = None
            for n in sorted({frame for frame, _ in blocks}):
                mine = sum(
                    jnp.where(block == k, table, 0.0)
                    for k, (frame, _) in enumerate(blocks)
                    if frame == n
                )
                term = dot_exact(joint[n], mine)
                picked = term if picked is None else picked + term
            wide = jnp.broadcast_to(picked[:, None, :], (32, 8, width)).reshape(256, width)
            total = jnp.where(gap == a, wide, total)
        high = total.astype(BF16).astype(F32)
        for k, (_, rest) in enumerate(blocks):
            if rest:
                inside = (at >= 96 * k) & (at < 96 * k + 96)
                high = jnp.where(inside, total - high, high)
        return high.astype(BF16)

    near = build(((0, False), (0, True), (1, False), (1, False), (1, True)))
    far = build(((2, False), (2, True)))
    return near, far


def near_kernel(core_ref, own_ref, temporal_ref, spatial_ref, acc_ref, far_ref, lay, m_ref):
    m_ref[...], far_ref[...] = mixing_matrices(temporal_ref, spatial_ref)
    spread(lay, [core_ref[...].astype(F32), own_ref[...]])
    for i in range(SIDE // 8):
        near = lay[0:6, 8 * i : 8 * i + 16, :].reshape(6 * 16, SIDE).astype(BF16)
        window = lay[6:12, 8 * i : 8 * i + 16, :].reshape(6 * 16, SIDE)
        high = window.astype(BF16)
        low = (window - high.astype(F32)).astype(BF16)
        acc_ref[i] = dot_nn(m_ref[...], jnp.concatenate([near, near, high, low, high], 0))


def refine_kernel(chip_ref, own_ref, acc_ref, m_ref, p_ref, out_hbm, lay, out_ref, sems):
    spread(lay, [chip_ref[...].astype(F32)])
    steps = SIDE // 8
    copies = []
    for i in range(steps):
        window = lay[:, 8 * i : 8 * i + 16, :].reshape(6 * 16, SIDE).astype(BF16)
        mix = dot_nn(m_ref[...], jnp.concatenate([window, window], 0)) + acc_ref[i]
        re = None
        im = None
        for o in range(32):
            v = jnp.maximum(mix[8 * o : 8 * o + 8], 0.0)
            re = v * p_ref[0, o] if re is None else re + v * p_ref[0, o]
            im = v * p_ref[1, o] if im is None else im + v * p_ref[1, o]
        rows = slice(8 * i, 8 * i + 8)
        out_ref[rows, :] = own_ref[rows, :] + jnp.concatenate([re, im], 1)
        if i % 6 == 5:
            part = pl.ds(8 * (i - 5), 48)
            copies.append(
                pltpu.make_async_copy(out_ref.at[part], out_hbm.at[part], sems.at[i // 6])
            )
            copies[-1].start()
    for copy in copies:
        copy.wait()


def params(mib):
    return pltpu.CompilerParams(vmem_limit_bytes=mib * 1024 * 1024)


def groups(cuts, frames):
    found = {}
    for c in range(cuts):
        for f in range(frames):
            found.setdefault((c % (cuts // MB), f // G), []).append(c * frames + f)
    return list(found.values())


def cost(flops, moved):
    return pl.CostEstimate(flops=flops, bytes_accessed=moved, transcendentals=0)


def on_device(
    cine_image,
    coil_maps,
    caipi_shift,
    line_mask,
    measured,
    spatial_weight,
    temporal_weight,
    project_weight,
):
    cuts = lax.axis_size("cuts")
    frames = lax.axis_size("frame")
    image = cine_image[0, 0]
    send = pl.pallas_call(
        pack_kernel,
        out_shape=jax.ShapeDtypeStruct((PEERS, CHUNK, 2 * SIDE), BF16),
        in_specs=[SMEM, HBM, HBM, HBM, HBM, HBM],
        out_specs=HBM,
        scratch_shapes=[
            pltpu.VMEM((SIDE, 2 * SIDE), F32),
            pltpu.VMEM((PER, SIDE, 2 * SIDE), BF16),
            pltpu.VMEM((COILS, QR, 2 * SIDE), BF16),
            pltpu.VMEM((1, SIDE), jnp.int32),
            pltpu.VMEM((4 * SIDE, 2 * SIDE), BF16),
            pltpu.VMEM((8, SIDE, 2 * SIDE), F32),
            pltpu.VMEM((PEERS, CHUNK, 2 * SIDE), BF16),
            pltpu.SemaphoreType.DMA((5,)),
            pltpu.SemaphoreType.DMA((PEERS,)),
        ],
        compiler_params=params(58),
        name="pack",
    )(
        caipi_shift,
        image,
        coil_maps[0],
        measured[0, 0],
        line_mask,
        jnp.asarray(width_matrix()),
    )
    where = groups(cuts, frames)
    got = lax.all_to_all(send, ("cuts", "frame"), 0, 0, axis_index_groups=where)
    slab = pl.pallas_call(
        slab_kernel,
        out_shape=jax.ShapeDtypeStruct((PEERS, 2 * SLAB, 2 * SIDE), BF16),
        in_specs=[VMEM, VMEM],
        out_specs=HBM,
        scratch_shapes=[
            pltpu.VMEM((PEERS, 2, 8, 512), F32),
            pltpu.VMEM((PEERS, 5, 8, 512), F32),
            pltpu.VMEM((MB, 40 * G, 2 * SIDE), F32),
            pltpu.VMEM((MB, 40 * G, 512), F32),
            pltpu.VMEM((PEERS, 2 * SLAB, 2 * SIDE), BF16),
            pltpu.SemaphoreType.DMA((PEERS,)),
        ],
        compiler_params=params(32),
        name="slab",
    )(got, jnp.asarray(slab_matrices()))
    back = lax.all_to_all(slab, ("cuts", "frame"), 0, 0, axis_index_groups=where)
    updated, edge = pl.pallas_call(
        update_kernel,
        out_shape=(
            jax.ShapeDtypeStruct((SIDE, 2 * SIDE), F32),
            jax.ShapeDtypeStruct((SIDE, 2 * SIDE), BF16),
        ),
        in_specs=[SMEM, VMEM, VMEM],
        out_specs=(VMEM, VMEM),
        scratch_shapes=[pltpu.VMEM((SIDE, 2 * SIDE), F32), pltpu.VMEM((SIDE, 2 * SIDE), F32)],
        compiler_params=params(16),
        name="update",
    )(caipi_shift, image, back)
    on_chip = lax.ppermute(edge, "frame", [(i, i ^ 1) for i in range(frames)])
    off_chip = lax.ppermute(
        edge, "frame", [(i, (i + 1) % frames if i % 2 else (i - 1) % frames) for i in range(frames)]
    )
    mixed, far_matrix = pl.pallas_call(
        near_kernel,
        out_shape=(
            jax.ShapeDtypeStruct((SIDE // 8, 256, SIDE), F32),
            jax.ShapeDtypeStruct((256, 192), BF16),
        ),
        in_specs=[VMEM, VMEM, VMEM, VMEM],
        out_specs=(VMEM, VMEM),
        scratch_shapes=[pltpu.VMEM((12, 208, SIDE), F32), pltpu.VMEM((256, 480), BF16)],
        compiler_params=params(24),
        cost_estimate=cost(24 * 2 * 256 * 480 * 192, 6 * 2**20),
        name="near",
    )(on_chip, updated, temporal_weight, spatial_weight.reshape(32, 18))
    refined = pl.pallas_call(
        refine_kernel,
        out_shape=jax.ShapeDtypeStruct((SIDE, 2 * SIDE), F32),
        in_specs=[VMEM, VMEM, VMEM, VMEM, SMEM],
        out_specs=HBM,
        scratch_shapes=[
            pltpu.VMEM((6, 208, SIDE), F32),
            pltpu.VMEM((SIDE, 2 * SIDE), F32),
            pltpu.SemaphoreType.DMA((4,)),
        ],
        compiler_params=params(24),
        name="refine",
    )(off_chip, updated, mixed, far_matrix, project_weight)
    return refined[None, None]


def solution(mesh):
    return jax.shard_map(
        on_device,
        mesh=mesh,
        in_specs=(
            P("cuts", "frame", None, None),
            P("cuts", None, None, None),
            P("cuts"),
            P("frame", None),
            P("cuts", "frame", None, None, None),
            P(),
            P(),
            P(),
        ),
        out_specs=P("cuts", "frame", None, None),
        check_vma=False,
    )
```

```python
import math

import jax
import jax.numpy as jnp
import ml_dtypes
import numpy as np
from jax import lax
from jax.experimental import pallas as pl
from jax.experimental.pallas import tpu as pltpu
from jax.sharding import PartitionSpec as P


MB = 4
G = 4
PEERS = MB * G
SIDE = 192
COILS = 12
PER = COILS // MB
QR = SIDE // MB
SLAB = SIDE // PEERS
CHUNK = 88
MARK = 1e30
F32 = jnp.float32
BF16 = jnp.bfloat16
VMEM = pl.BlockSpec(memory_space=pltpu.VMEM)
SMEM = pl.BlockSpec(memory_space=pltpu.SMEM)
ANY = pl.BlockSpec(memory_space=pl.ANY)
HBM = pl.BlockSpec(memory_space=pltpu.HBM)


def hi_lo(table):
    high = table.astype(ml_dtypes.bfloat16)
    low = (table - high.astype(np.float64)).astype(ml_dtypes.bfloat16)
    return high, low


def tables():
    at = np.arange(SIDE)
    angle = (at[:, None] * at[None, :] % SIDE) * (2.0 * math.pi / SIDE)
    cos = np.cos(angle) / math.sqrt(SIDE)
    sin = np.sin(angle) / math.sqrt(SIDE)
    return cos, sin


def width_matrix():
    cos, sin = tables()
    both = np.concatenate([np.concatenate([cos, -sin], 1), np.concatenate([sin, cos], 1)], 0)
    high, low = hi_lo(both)
    return np.concatenate([high, low], 0)


def folded(re, im):
    return np.concatenate([re[:, :128], re[:, 128:], im[:, 128:], im[:, :128]], 1)


def height_matrix():
    cos, sin = tables()
    real = folded(cos, sin)
    imag = folded(-sin, cos)
    both = np.concatenate([real, real, imag, imag], 0)
    return np.stack(hi_lo(both))


def line_pieces(group):
    off = QR * ((MB - group) % MB)
    return ((off, 128), (off + 128, 64), (2 * SIDE + off + 128, 64), (2 * SIDE + off, 128))


def slab_matrices():
    table = height_matrix()
    turned = []
    for j in range(MB):
        rows = np.concatenate([table[:, s : s + n] for s, n in line_pieces(j)], 1)
        turned.append(np.swapaxes(rows, 1, 2))
    return np.stack(turned + [table[:, : 2 * SIDE], table[:, 2 * SIDE :]])


def fold(re, im):
    return jnp.concatenate([re[:, :128], re[:, 128:], im[:, 128:], im[:, :128]], 1)


def dot_nt(a, b):
    return lax.dot_general(a, b, (((1,), (1,)), ((), ())), preferred_element_type=F32)


def dot_nn(a, b):
    return lax.dot_general(a, b, (((1,), (0,)), ((), ())), preferred_element_type=F32)


def pack_kernel(
    turn_hbm, x_hbm, maps_hbm, meas_hbm, mask_hbm, w_hbm, out_hbm,
    turn_ref, x_ref, maps_ref, meas_ref, mask_ref, w_ref, parts, out_ref, sems, out_sems,
):
    quarter = lax.axis_index("cuts") // (lax.axis_size("cuts") // MB)
    member = lax.rem(lax.axis_index("frame"), G)
    loads = [
        pltpu.make_async_copy(src, dst, sems.at[n])
        for n, (src, dst) in enumerate(
            (
                (x_hbm, x_ref),
                (maps_hbm.at[pl.ds(member * PER, PER)], maps_ref),
                (mask_hbm, mask_ref),
                (w_hbm, w_ref),
                (meas_hbm, meas_ref),
                (turn_hbm, turn_ref),
            )
        )
    ]
    for load in loads:
        load.start()
    loads[5].wait()
    turn = turn_ref[0]

    def start(block):
        return pl.multiple_of(lax.rem(turn + block, MB) * QR, 16)

    loads[0].wait()
    flipped = jnp.concatenate([x_ref[pl.ds(start(b), QR), :] for b in range(MB)], 0).T
    image = fold(flipped[:SIDE], flipped[SIDE:])
    high = image.astype(BF16).astype(F32)
    parts[3] = high
    parts[7] = image - high
    loads[1].wait()
    for r in range(PER):
        flipped = jnp.concatenate(
            [maps_ref[r, pl.ds(start(b), QR), :] for b in range(MB)], 0
        ).astype(F32).T
        parts[r] = fold(flipped[:SIDE], flipped[SIDE:])
    lane = lax.broadcasted_iota(jnp.int32, (SIDE, 2 * SIDE), 1)
    line = jnp.where(lane < SIDE, lane, jnp.where(lane < 256, lane - 64, lane - 256))
    for _ in range(MB - 1):
        line = jnp.where(line >= QR, line - QR, line)
    lines = lax.broadcasted_iota(jnp.int32, (SIDE, 2 * SIDE), 0)
    select = (lines == line + quarter * QR).astype(F32).astype(BF16)
    loads[2].wait()
    mask8 = jnp.broadcast_to(mask_ref[...].astype(F32), (8, SIDE)).astype(BF16)
    sampled = dot_nn(mask8, select)[0:1] > 0.5
    loads[3].wait()
    loads[4].wait()
    for r in range(PER):
        rows = [meas_ref[PER * lax.rem(p + MB - quarter, MB) + r] for p in range(MB)]
        both = dot_nt(w_ref[...], jnp.concatenate(rows, 0))
        re = both[0:SIDE] + both[2 * SIDE : 3 * SIDE]
        im = both[SIDE : 2 * SIDE] + both[3 * SIDE :]
        parts[4 + r] = jnp.where(sampled, fold(re, im), MARK)
    for i in range(PEERS):
        tiles = [parts[p, 8 * i : 8 * i + 8, :] for p in range(7)]
        tiles += [parts[p, 128 + 4 * i : 132 + 4 * i, :] for p in range(8)]
        out_ref[i] = jnp.concatenate(tiles, 0).astype(BF16)
        pltpu.make_async_copy(out_ref.at[i], out_hbm.at[i], out_sems.at[i]).start()
    for i in range(PEERS):
        pltpu.make_async_copy(out_ref.at[i], out_hbm.at[i], out_sems.at[i]).wait()


def cut(value):
    return [value[8 * t : 8 * t + 8] for t in range(value.shape[0] // 8)]


def slab_kernel(got_ref, a_ref, out_hbm, xs, cs, zs, ys, out_ref, sems):
    left = lax.broadcasted_iota(jnp.int32, (8, 128), 1) < 64
    lane = lax.broadcasted_iota(jnp.int32, (8, 128), 1)
    low16 = (lane < 16) | ((lane >= 64) & (lane < 80))
    for i in range(PEERS):
        tiles = cut(got_ref[i].astype(F32))
        x4 = (tiles[8] + tiles[10])[4:8]
        for t, x in enumerate((tiles[3], jnp.concatenate([x4, x4], 0))):
            mid = x[:, 128:256]
            turned = pltpu.roll(mid, 64, 1)
            xs[i, t, :, 0:128] = x[:, 0:128]
            xs[i, t, :, 128:256] = jnp.where(left, mid, turned)
            xs[i, t, :, 256:384] = jnp.where(left, -turned, mid)
            xs[i, t, :, 384:512] = x[:, 256:384]
        for t, c in enumerate(tiles[0:3] + tiles[7:9]):
            cs[i, t, :, 0:384] = c
            cs[i, t, :, 384:512] = pltpu.roll(c[:, 128:256], 64, 1)

    def gather(j):
        for t in range(5):
            acc = [None] * G
            for m in range(MB):
                c0, c1, c2, c1t = (cs[m * G + j, t, :, 128 * n : 128 * n + 128] for n in range(4))
                for f in range(G):
                    x0, xa, xb, x2 = (
                        xs[m * G + f, t // 3, :, 128 * n : 128 * n + 128] for n in range(4)
                    )
                    o = (c0 * x0 - c2 * x2, c1 * xa + c1t * xb, c0 * x2 + c2 * x0)
                    acc[f] = o if m == 0 else tuple(p + q for p, q in zip(acc[f], o))
            for f in range(G):
                for n in range(3):
                    zs[j, 40 * f + 8 * t : 40 * f + 8 * t + 8, 128 * n : 128 * n + 128] = acc[f][n]

    def matrices(j):
        return [
            jnp.concatenate(
                [
                    a_ref[MB + s // (2 * SIDE), h, s % (2 * SIDE) : s % (2 * SIDE) + n, :]
                    for s, n in line_pieces(j)
                ],
                0,
            )
            for h in range(2)
        ]

    def triple(value, high, low):
        top = value.astype(BF16)
        rest = (value - top.astype(F32)).astype(BF16)
        return dot_nn(
            jnp.concatenate([top, rest, top], 1), jnp.concatenate([high, high, low], 0)
        )

    def residual(j, zk):
        out = []
        for f in range(G):
            sources = []
            for p in range(MB):
                i = ((p - j) % MB) * G + f
                tiles = cut(got_ref[i].astype(F32))
                sources.append(tiles[4:7] + tiles[9:11])
            for t in range(5):
                row = 40 * f + 8 * t
                s0, s1, s2, s3 = (source[t] for source in sources)
                outer = [
                    jnp.where(lane < 48, s0[:, n], jnp.where(lane < 96, s1[:, n], s2[:, n]))
                    for n in (slice(0, 128), slice(256, 384))
                ]
                mid = jnp.where(low16, s2[:, 128:256], s3[:, 128:256])
                target = jnp.concatenate([outer[0], mid, outer[1]], 1)
                out.append(jnp.where(target > 0.1 * MARK, 0.0, zk[row : row + 8] - target))
        return jnp.concatenate(out, 0)

    gather(0)
    for j in range(MB):
        zk = triple(zs[j], a_ref[j, 0], a_ref[j, 1])
        if j + 1 < MB:
            gather(j + 1)
        y = triple(residual(j, zk), *matrices(j))
        ys[j, :, 0:384] = y
        ys[j, :, 384:512] = pltpu.roll(y[:, 128:256], 64, 1)

    for m in range(MB):
        sums = []
        for tiles in ((0, 1, 2), (3,), (4,)):
            acc = [None] * G
            for t in tiles:
                for j in range(MB):
                    c0, c1, c2, c1t = (
                        cs[m * G + j, t, :, 128 * n : 128 * n + 128] for n in range(4)
                    )
                    ca = jnp.where(left, c1, c1t)
                    cb = jnp.where(left, c1t, -c1)
                    for f in range(G):
                        row = 40 * f + 8 * t
                        y0, y1, y2, y1t = (
                            ys[j, row : row + 8, 128 * n : 128 * n + 128] for n in range(4)
                        )
                        o = (c0 * y0 + c2 * y2, ca * y1 + cb * y1t, c0 * y2 - c2 * y0)
                        acc[f] = o if acc[f] is None else tuple(p + q for p, q in zip(acc[f], o))
            sums.append([jnp.concatenate(o, 1) for o in acc])
        for f in range(G):
            i = m * G + f
            main, third, fourth = (part[f] for part in sums)
            half = third[0:4] + third[4:8] + fourth[0:4]
            main_hi = main.astype(BF16).astype(F32)
            half_hi = half.astype(BF16).astype(F32)
            out_ref[i] = jnp.concatenate(
                [main_hi, main - main_hi, half_hi, half - half_hi], 0
            ).astype(BF16)
            pltpu.make_async_copy(out_ref.at[i], out_hbm.at[i], sems.at[i]).start()
    for i in range(PEERS):
        pltpu.make_async_copy(out_ref.at[i], out_hbm.at[i], sems.at[i]).wait()


def lost_part(x, mask, maps_ref):
    power = None
    for c in range(COILS):
        maps = maps_ref[c].astype(F32)
        power = maps * maps if power is None else power + maps * maps
    share = jnp.sum(mask.astype(F32), axis=1, keepdims=True) * (1.0 / SIDE)
    power = power + pltpu.roll(power, SIDE, 1)
    lane = lax.broadcasted_iota(jnp.int32, (SIDE, 2 * SIDE), 1)
    rounded = (lane < 128) | ((lane >= SIDE) & (lane < SIDE + 128))
    return share * power * jnp.where(rounded, x - x.astype(BF16).astype(F32), 0.0)


def update_kernel(turn_ref, x_ref, back_ref, out_ref, edge_ref, turned, grad):
    turn = turn_ref[0]
    for i in range(PEERS):
        both = back_ref[i].astype(F32)
        turned[8 * i : 8 * i + 8, :] = both[0:8] + both[8:16]
        turned[128 + 4 * i : 132 + 4 * i, :] = both[16:20] + both[20:24]
    re = turned[:, 0:SIDE]
    im = jnp.concatenate([turned[:, 256:384], turned[:, 192:256]], 1)
    grad[...] = jnp.concatenate([re, im], 0).T
    for b in range(MB):
        at = pl.multiple_of(lax.rem(b + MB - turn, MB) * QR, 16)
        rows = slice(b * QR, (b + 1) * QR)
        u = x_ref[rows, :] - 0.5 * grad[pl.ds(at, QR), :]
        out_ref[rows, :] = u
        edge_ref[rows, :] = u.astype(BF16)


def spread(lay, frames):
    zeros = jnp.zeros((lay.shape[0], 8, SIDE), F32)
    lay[:, 0:8, :] = zeros
    lay[:, 192:200, :] = zeros
    column = lax.broadcasted_iota(jnp.int32, (SIDE, SIDE), 1)
    for t, u in enumerate(frames):
        for p in range(2):
            for b in range(3):
                by = (1 - b - SIDE * p) % (2 * SIDE)
                v = (pltpu.roll(u, by, 1) if by else u)[:, :SIDE]
                if b == 0:
                    v = jnp.where(column == 0, 0.0, v)
                if b == 2:
                    v = jnp.where(column == SIDE - 1, 0.0, v)
                lay[(t * 2 + p) * 3 + b, 1 : SIDE + 1, :] = v


def dot_exact(a, b):
    return lax.dot_general(
        a, b, (((1,), (0,)), ((), ())), precision=lax.Precision.HIGHEST, preferred_element_type=F32
    )


def mixing_matrices(temporal_ref, spatial_ref):
    odd = lax.rem(lax.axis_index("frame"), 2) == 1
    before, after = temporal_ref[0], temporal_ref[2]
    joint = [
        dot_exact(side, spatial_ref[...])
        for side in (
            jnp.where(odd, before, after),
            temporal_ref[1],
            jnp.where(odd, after, before),
        )
    ]

    def build(blocks):
        width = 96 * len(blocks)
        lane = lax.broadcasted_iota(jnp.int32, (18, width), 1)
        entry = lax.broadcasted_iota(jnp.int32, (18, width), 0)
        block = sum((lane >= 96 * n).astype(jnp.int32) for n in range(1, len(blocks)))
        channel = (lane - 96 * block) >> 4
        part = (channel >= 3).astype(jnp.int32)
        at = lax.broadcasted_iota(jnp.int32, (256, width), 1)
        gap = (at & 15) - (lax.broadcasted_iota(jnp.int32, (256, width), 0) & 7)
        total = jnp.zeros((256, width), F32)
        for a in range(3):
            table = (entry == part * 6 + a * 3 + channel).astype(F32)
            picked = None
            for n in sorted({frame for frame, _ in blocks}):
                mine = sum(
                    jnp.where(block == k, table, 0.0)
                    for k, (frame, _) in enumerate(blocks)
                    if frame == n
                )
                term = dot_exact(joint[n], mine)
                picked = term if picked is None else picked + term
            wide = jnp.broadcast_to(picked[:, None, :], (32, 8, width)).reshape(256, width)
            total = jnp.where(gap == a, wide, total)
        high = total.astype(BF16).astype(F32)
        for k, (_, rest) in enumerate(blocks):
            if rest:
                inside = (at >= 96 * k) & (at < 96 * k + 96)
                high = jnp.where(inside, total - high, high)
        return high.astype(BF16)

    near = build(((0, False), (0, True), (1, False), (1, False), (1, True)))
    far = build(((2, False), (2, True)))
    return near, far


def near_kernel(
    core_ref, own_ref, x_ref, mask_ref, temporal_ref, spatial_ref, maps_ref,
    acc_ref, far_ref, out_ref, lay, m_ref,
):
    m_ref[...], far_ref[...] = mixing_matrices(temporal_ref, spatial_ref)
    own = own_ref[...] - 0.5 * lost_part(x_ref[...], mask_ref[...], maps_ref)
    out_ref[...] = own
    spread(lay, [core_ref[...].astype(F32), own])
    for i in range(SIDE // 8):
        near = lay[0:6, 8 * i : 8 * i + 16, :].reshape(6 * 16, SIDE).astype(BF16)
        window = lay[6:12, 8 * i : 8 * i + 16, :].reshape(6 * 16, SIDE)
        high = window.astype(BF16)
        low = (window - high.astype(F32)).astype(BF16)
        acc_ref[i] = dot_nn(m_ref[...], jnp.concatenate([near, near, high, low, high], 0))


def refine_kernel(chip_ref, own_ref, acc_ref, m_ref, p_ref, out_hbm, lay, out_ref, sems):
    spread(lay, [chip_ref[...].astype(F32)])
    steps = SIDE // 8
    copies = []
    for i in range(steps):
        window = lay[:, 8 * i : 8 * i + 16, :].reshape(6 * 16, SIDE).astype(BF16)
        mix = dot_nn(m_ref[...], jnp.concatenate([window, window], 0)) + acc_ref[i]
        re = None
        im = None
        for o in range(32):
            v = jnp.maximum(mix[8 * o : 8 * o + 8], 0.0)
            re = v * p_ref[0, o] if re is None else re + v * p_ref[0, o]
            im = v * p_ref[1, o] if im is None else im + v * p_ref[1, o]
        rows = slice(8 * i, 8 * i + 8)
        out_ref[rows, :] = own_ref[rows, :] + jnp.concatenate([re, im], 1)
        if i % 6 == 5:
            part = pl.ds(8 * (i - 5), 48)
            copies.append(
                pltpu.make_async_copy(out_ref.at[part], out_hbm.at[part], sems.at[i // 6])
            )
            copies[-1].start()
    for copy in copies:
        copy.wait()


def params(mib):
    return pltpu.CompilerParams(vmem_limit_bytes=mib * 1024 * 1024)


def groups(cuts, frames):
    found = {}
    for c in range(cuts):
        for f in range(frames):
            found.setdefault((c % (cuts // MB), f // G), []).append(c * frames + f)
    return list(found.values())


def cost(flops, moved):
    return pl.CostEstimate(flops=flops, bytes_accessed=moved, transcendentals=0)


def on_device(
    cine_image,
    coil_maps,
    caipi_shift,
    line_mask,
    measured,
    spatial_weight,
    temporal_weight,
    project_weight,
):
    cuts = lax.axis_size("cuts")
    frames = lax.axis_size("frame")
    image = cine_image[0, 0]
    send = pl.pallas_call(
        pack_kernel,
        out_shape=jax.ShapeDtypeStruct((PEERS, CHUNK, 2 * SIDE), BF16),
        in_specs=[HBM, HBM, HBM, HBM, HBM, HBM],
        out_specs=HBM,
        scratch_shapes=[
            pltpu.SMEM((1,), jnp.int32),
            pltpu.VMEM((SIDE, 2 * SIDE), F32),
            pltpu.VMEM((PER, SIDE, 2 * SIDE), BF16),
            pltpu.VMEM((COILS, QR, 2 * SIDE), BF16),
            pltpu.VMEM((1, SIDE), jnp.int32),
            pltpu.VMEM((4 * SIDE, 2 * SIDE), BF16),
            pltpu.VMEM((8, SIDE, 2 * SIDE), F32),
            pltpu.VMEM((PEERS, CHUNK, 2 * SIDE), BF16),
            pltpu.SemaphoreType.DMA((6,)),
            pltpu.SemaphoreType.DMA((PEERS,)),
        ],
        compiler_params=params(58),
        name="pack",
    )(
        caipi_shift,
        image,
        coil_maps[0],
        measured[0, 0],
        line_mask,
        jnp.asarray(width_matrix()),
    )
    where = groups(cuts, frames)
    got = lax.all_to_all(send, ("cuts", "frame"), 0, 0, axis_index_groups=where)
    slab = pl.pallas_call(
        slab_kernel,
        out_shape=jax.ShapeDtypeStruct((PEERS, 2 * SLAB, 2 * SIDE), BF16),
        in_specs=[VMEM, VMEM],
        out_specs=HBM,
        scratch_shapes=[
            pltpu.VMEM((PEERS, 2, 8, 512), F32),
            pltpu.VMEM((PEERS, 5, 8, 512), F32),
            pltpu.VMEM((MB, 40 * G, 2 * SIDE), F32),
            pltpu.VMEM((MB, 40 * G, 512), F32),
            pltpu.VMEM((PEERS, 2 * SLAB, 2 * SIDE), BF16),
            pltpu.SemaphoreType.DMA((PEERS,)),
        ],
        compiler_params=params(32),
        name="slab",
    )(got, jnp.asarray(slab_matrices()))
    back = lax.all_to_all(slab, ("cuts", "frame"), 0, 0, axis_index_groups=where)
    updated, edge = pl.pallas_call(
        update_kernel,
        out_shape=(
            jax.ShapeDtypeStruct((SIDE, 2 * SIDE), F32),
            jax.ShapeDtypeStruct((SIDE, 2 * SIDE), BF16),
        ),
        in_specs=[SMEM, VMEM, VMEM],
        out_specs=(VMEM, VMEM),
        scratch_shapes=[pltpu.VMEM((SIDE, 2 * SIDE), F32), pltpu.VMEM((SIDE, 2 * SIDE), F32)],
        compiler_params=params(16),
        name="update",
    )(caipi_shift, image, back)
    on_chip = lax.ppermute(edge, "frame", [(i, i ^ 1) for i in range(frames)])
    off_chip = lax.ppermute(
        edge, "frame", [(i, (i + 1) % frames if i % 2 else (i - 1) % frames) for i in range(frames)]
    )
    mixed, far_matrix, own = pl.pallas_call(
        near_kernel,
        out_shape=(
            jax.ShapeDtypeStruct((SIDE // 8, 256, SIDE), F32),
            jax.ShapeDtypeStruct((256, 192), BF16),
            jax.ShapeDtypeStruct((SIDE, 2 * SIDE), F32),
        ),
        in_specs=[VMEM, VMEM, VMEM, VMEM, VMEM, VMEM, VMEM],
        out_specs=(VMEM, VMEM, VMEM),
        scratch_shapes=[
            pltpu.VMEM((12, 208, SIDE), F32),
            pltpu.VMEM((256, 480), BF16),
        ],
        compiler_params=params(24),
        cost_estimate=cost(24 * 2 * 256 * 480 * 192, 6 * 2**20),
        name="near",
    )(
        on_chip,
        updated,
        image,
        line_mask,
        temporal_weight,
        spatial_weight.reshape(32, 18),
        coil_maps[0],
    )
    refined = pl.pallas_call(
        refine_kernel,
        out_shape=jax.ShapeDtypeStruct((SIDE, 2 * SIDE), F32),
        in_specs=[VMEM, VMEM, VMEM, VMEM, SMEM],
        out_specs=HBM,
        scratch_shapes=[
            pltpu.VMEM((6, 208, SIDE), F32),
            pltpu.VMEM((SIDE, 2 * SIDE), F32),
            pltpu.SemaphoreType.DMA((4,)),
        ],
        compiler_params=params(24),
        name="refine",
    )(off_chip, own, mixed, far_matrix, project_weight)
    return refined[None, None]


def solution(mesh):
    return jax.shard_map(
        on_device,
        mesh=mesh,
        in_specs=(
            P("cuts", "frame", None, None),
            P("cuts", None, None, None),
            P("cuts"),
            P("frame", None),
            P("cuts", "frame", None, None, None),
            P(),
            P(),
            P(),
        ),
        out_specs=P("cuts", "frame", None, None),
        check_vma=False,
    )
```

```python
import math

import jax
import jax.numpy as jnp
import ml_dtypes
import numpy as np
from jax import lax
from jax.experimental import pallas as pl
from jax.experimental.pallas import tpu as pltpu
from jax.sharding import PartitionSpec as P


MB = 4
G = 4
PEERS = MB * G
SIDE = 192
COILS = 12
PER = COILS // MB
QR = SIDE // MB
SLAB = SIDE // PEERS
CHUNK = 88
MARK = 1e30
F32 = jnp.float32
BF16 = jnp.bfloat16
VMEM = pl.BlockSpec(memory_space=pltpu.VMEM)
SMEM = pl.BlockSpec(memory_space=pltpu.SMEM)
ANY = pl.BlockSpec(memory_space=pl.ANY)
HBM = pl.BlockSpec(memory_space=pltpu.HBM)


def hi_lo(table):
    high = table.astype(ml_dtypes.bfloat16)
    low = (table - high.astype(np.float64)).astype(ml_dtypes.bfloat16)
    return high, low


def tables():
    at = np.arange(SIDE)
    angle = (at[:, None] * at[None, :] % SIDE) * (2.0 * math.pi / SIDE)
    cos = np.cos(angle) / math.sqrt(SIDE)
    sin = np.sin(angle) / math.sqrt(SIDE)
    return cos, sin


def width_matrix():
    cos, sin = tables()
    both = np.concatenate([np.concatenate([cos, -sin], 1), np.concatenate([sin, cos], 1)], 0)
    high, low = hi_lo(both)
    return np.concatenate([high, low], 0)


def folded(re, im):
    return np.concatenate([re[:, :128], re[:, 128:], im[:, 128:], im[:, :128]], 1)


def height_matrix():
    cos, sin = tables()
    real = folded(cos, sin)
    imag = folded(-sin, cos)
    both = np.concatenate([real, real, imag, imag], 0)
    return np.stack(hi_lo(both))


def line_pieces(group):
    off = QR * ((MB - group) % MB)
    return ((off, 128), (off + 128, 64), (2 * SIDE + off + 128, 64), (2 * SIDE + off, 128))


def slab_matrices():
    table = height_matrix()
    turned = []
    for j in range(MB):
        rows = np.concatenate([table[:, s : s + n] for s, n in line_pieces(j)], 1)
        turned.append(np.swapaxes(rows, 1, 2))
    return np.stack(turned + [table[:, : 2 * SIDE], table[:, 2 * SIDE :]])


def fold(re, im):
    return jnp.concatenate([re[:, :128], re[:, 128:], im[:, 128:], im[:, :128]], 1)


def dot_nt(a, b):
    return lax.dot_general(a, b, (((1,), (1,)), ((), ())), preferred_element_type=F32)


def dot_nn(a, b):
    return lax.dot_general(a, b, (((1,), (0,)), ((), ())), preferred_element_type=F32)


def pack_kernel(
    turn_hbm, x_hbm, maps_hbm, meas_hbm, mask_hbm, w_hbm, out_hbm,
    turn_ref, x_ref, maps_ref, meas_ref, mask_ref, w_ref, parts, out_ref, sems, out_sems,
):
    quarter = lax.axis_index("cuts") // (lax.axis_size("cuts") // MB)
    member = lax.rem(lax.axis_index("frame"), G)
    loads = [
        pltpu.make_async_copy(src, dst, sems.at[n])
        for n, (src, dst) in enumerate(
            (
                (x_hbm, x_ref),
                (maps_hbm.at[pl.ds(member * PER, PER)], maps_ref),
                (mask_hbm, mask_ref),
                (w_hbm, w_ref),
                (meas_hbm, meas_ref),
                (turn_hbm, turn_ref),
            )
        )
    ]
    for load in loads:
        load.start()
    loads[5].wait()
    turn = turn_ref[0]

    def start(block):
        return pl.multiple_of(lax.rem(turn + block, MB) * QR, 16)

    loads[0].wait()
    flipped = jnp.concatenate([x_ref[pl.ds(start(b), QR), :] for b in range(MB)], 0).T
    image = fold(flipped[:SIDE], flipped[SIDE:])
    high = image.astype(BF16).astype(F32)
    parts[3] = high
    parts[7] = image - high
    loads[1].wait()
    for r in range(PER):
        flipped = jnp.concatenate(
            [maps_ref[r, pl.ds(start(b), QR), :] for b in range(MB)], 0
        ).astype(F32).T
        parts[r] = fold(flipped[:SIDE], flipped[SIDE:])
    lane = lax.broadcasted_iota(jnp.int32, (SIDE, 2 * SIDE), 1)
    line = jnp.where(lane < SIDE, lane, jnp.where(lane < 256, lane - 64, lane - 256))
    for _ in range(MB - 1):
        line = jnp.where(line >= QR, line - QR, line)
    lines = lax.broadcasted_iota(jnp.int32, (SIDE, 2 * SIDE), 0)
    select = (lines == line + quarter * QR).astype(F32).astype(BF16)
    loads[2].wait()
    mask8 = jnp.broadcast_to(mask_ref[...].astype(F32), (8, SIDE)).astype(BF16)
    sampled = dot_nn(mask8, select)[0:1] > 0.5
    loads[3].wait()
    loads[4].wait()
    for r in range(PER):
        rows = [meas_ref[PER * lax.rem(p + MB - quarter, MB) + r] for p in range(MB)]
        both = dot_nt(w_ref[...], jnp.concatenate(rows, 0))
        re = both[0:SIDE] + both[2 * SIDE : 3 * SIDE]
        im = both[SIDE : 2 * SIDE] + both[3 * SIDE :]
        parts[4 + r] = jnp.where(sampled, fold(re, im), MARK)
    for i in range(PEERS):
        tiles = [parts[p, 8 * i : 8 * i + 8, :] for p in range(7)]
        tiles += [parts[p, 128 + 4 * i : 132 + 4 * i, :] for p in range(8)]
        out_ref[i] = jnp.concatenate(tiles, 0).astype(BF16)
        pltpu.make_async_copy(out_ref.at[i], out_hbm.at[i], out_sems.at[i]).start()
    for i in range(PEERS):
        pltpu.make_async_copy(out_ref.at[i], out_hbm.at[i], out_sems.at[i]).wait()


def cut(value):
    return [value[8 * t : 8 * t + 8] for t in range(value.shape[0] // 8)]


def slab_kernel(got_ref, a_ref, out_ref, xs, cs, zs, ys):
    left = lax.broadcasted_iota(jnp.int32, (8, 128), 1) < 64
    lane = lax.broadcasted_iota(jnp.int32, (8, 128), 1)
    low16 = (lane < 16) | ((lane >= 64) & (lane < 80))
    for i in range(PEERS):
        tiles = cut(got_ref[i].astype(F32))
        x4 = (tiles[8] + tiles[10])[4:8]
        for t, x in enumerate((tiles[3], jnp.concatenate([x4, x4], 0))):
            mid = x[:, 128:256]
            turned = pltpu.roll(mid, 64, 1)
            xs[i, t, :, 0:128] = x[:, 0:128]
            xs[i, t, :, 128:256] = jnp.where(left, mid, turned)
            xs[i, t, :, 256:384] = jnp.where(left, -turned, mid)
            xs[i, t, :, 384:512] = x[:, 256:384]
        for t, c in enumerate(tiles[0:3] + tiles[7:9]):
            cs[i, t, :, 0:384] = c
            cs[i, t, :, 384:512] = pltpu.roll(c[:, 128:256], 64, 1)

    def gather(j):
        for t in range(5):
            acc = [None] * G
            for m in range(MB):
                c0, c1, c2, c1t = (cs[m * G + j, t, :, 128 * n : 128 * n + 128] for n in range(4))
                for f in range(G):
                    x0, xa, xb, x2 = (
                        xs[m * G + f, t // 3, :, 128 * n : 128 * n + 128] for n in range(4)
                    )
                    o = (c0 * x0 - c2 * x2, c1 * xa + c1t * xb, c0 * x2 + c2 * x0)
                    acc[f] = o if m == 0 else tuple(p + q for p, q in zip(acc[f], o))
            for f in range(G):
                for n in range(3):
                    zs[j, 40 * f + 8 * t : 40 * f + 8 * t + 8, 128 * n : 128 * n + 128] = acc[f][n]

    def matrices(j):
        return [
            jnp.concatenate(
                [
                    a_ref[MB + s // (2 * SIDE), h, s % (2 * SIDE) : s % (2 * SIDE) + n, :]
                    for s, n in line_pieces(j)
                ],
                0,
            )
            for h in range(2)
        ]

    def triple(value, high, low):
        top = value.astype(BF16)
        rest = (value - top.astype(F32)).astype(BF16)
        return dot_nn(
            jnp.concatenate([top, rest, top], 1), jnp.concatenate([high, high, low], 0)
        )

    def residual(j, zk):
        out = []
        for f in range(G):
            sources = []
            for p in range(MB):
                i = ((p - j) % MB) * G + f
                tiles = cut(got_ref[i].astype(F32))
                sources.append(tiles[4:7] + tiles[9:11])
            for t in range(5):
                row = 40 * f + 8 * t
                s0, s1, s2, s3 = (source[t] for source in sources)
                outer = [
                    jnp.where(lane < 48, s0[:, n], jnp.where(lane < 96, s1[:, n], s2[:, n]))
                    for n in (slice(0, 128), slice(256, 384))
                ]
                mid = jnp.where(low16, s2[:, 128:256], s3[:, 128:256])
                target = jnp.concatenate([outer[0], mid, outer[1]], 1)
                out.append(jnp.where(target > 0.1 * MARK, 0.0, zk[row : row + 8] - target))
        return jnp.concatenate(out, 0)

    gather(0)
    for j in range(MB):
        zk = triple(zs[j], a_ref[j, 0], a_ref[j, 1])
        if j + 1 < MB:
            gather(j + 1)
        y = triple(residual(j, zk), *matrices(j))
        ys[j, :, 0:384] = y
        ys[j, :, 384:512] = pltpu.roll(y[:, 128:256], 64, 1)

    for m in range(MB):
        sums = []
        for tiles in ((0, 1, 2), (3,), (4,)):
            acc = [None] * G
            for t in tiles:
                for j in range(MB):
                    c0, c1, c2, c1t = (
                        cs[m * G + j, t, :, 128 * n : 128 * n + 128] for n in range(4)
                    )
                    ca = jnp.where(left, c1, c1t)
                    cb = jnp.where(left, c1t, -c1)
                    for f in range(G):
                        row = 40 * f + 8 * t
                        y0, y1, y2, y1t = (
                            ys[j, row : row + 8, 128 * n : 128 * n + 128] for n in range(4)
                        )
                        o = (c0 * y0 + c2 * y2, ca * y1 + cb * y1t, c0 * y2 - c2 * y0)
                        acc[f] = o if acc[f] is None else tuple(p + q for p, q in zip(acc[f], o))
            sums.append([jnp.concatenate(o, 1) for o in acc])
        for f in range(G):
            i = m * G + f
            main, third, fourth = (part[f] for part in sums)
            half = third[0:4] + third[4:8] + fourth[0:4]
            main_hi = main.astype(BF16).astype(F32)
            half_hi = half.astype(BF16).astype(F32)
            out_ref[i] = jnp.concatenate(
                [main_hi, main - main_hi, half_hi, half - half_hi], 0
            ).astype(BF16)


def lost_part(x, mask, maps_ref):
    power = None
    for c in range(COILS):
        maps = maps_ref[c].astype(F32)
        power = maps * maps if power is None else power + maps * maps
    share = jnp.sum(mask.astype(F32), axis=1, keepdims=True) * (1.0 / SIDE)
    power = power + pltpu.roll(power, SIDE, 1)
    lane = lax.broadcasted_iota(jnp.int32, (SIDE, 2 * SIDE), 1)
    rounded = (lane < 128) | ((lane >= SIDE) & (lane < SIDE + 128))
    return share * power * jnp.where(rounded, x - x.astype(BF16).astype(F32), 0.0)


def update_kernel(turn_ref, x_ref, back_ref, out_ref, edge_ref, turned, grad):
    turn = turn_ref[0]
    for i in range(PEERS):
        both = back_ref[i].astype(F32)
        turned[8 * i : 8 * i + 8, :] = both[0:8] + both[8:16]
        turned[128 + 4 * i : 132 + 4 * i, :] = both[16:20] + both[20:24]
    re = turned[:, 0:SIDE]
    im = jnp.concatenate([turned[:, 256:384], turned[:, 192:256]], 1)
    grad[...] = jnp.concatenate([re, im], 0).T
    for b in range(MB):
        at = pl.multiple_of(lax.rem(b + MB - turn, MB) * QR, 16)
        rows = slice(b * QR, (b + 1) * QR)
        u = x_ref[rows, :] - 0.5 * grad[pl.ds(at, QR), :]
        out_ref[rows, :] = u
        edge_ref[rows, :] = u.astype(BF16)


def spread(lay, frames):
    zeros = jnp.zeros((lay.shape[0], 8, SIDE), F32)
    lay[:, 0:8, :] = zeros
    lay[:, 192:200, :] = zeros
    column = lax.broadcasted_iota(jnp.int32, (SIDE, SIDE), 1)
    for t, u in enumerate(frames):
        for p in range(2):
            for b in range(3):
                by = (1 - b - SIDE * p) % (2 * SIDE)
                v = (pltpu.roll(u, by, 1) if by else u)[:, :SIDE]
                if b == 0:
                    v = jnp.where(column == 0, 0.0, v)
                if b == 2:
                    v = jnp.where(column == SIDE - 1, 0.0, v)
                lay[(t * 2 + p) * 3 + b, 1 : SIDE + 1, :] = v


def dot_exact(a, b):
    return lax.dot_general(
        a, b, (((1,), (0,)), ((), ())), precision=lax.Precision.HIGHEST, preferred_element_type=F32
    )


def mixing_matrices(temporal_ref, spatial_ref):
    odd = lax.rem(lax.axis_index("frame"), 2) == 1
    before, after = temporal_ref[0], temporal_ref[2]
    joint = [
        dot_exact(side, spatial_ref[...])
        for side in (
            jnp.where(odd, before, after),
            temporal_ref[1],
            jnp.where(odd, after, before),
        )
    ]

    def build(blocks):
        width = 96 * len(blocks)
        lane = lax.broadcasted_iota(jnp.int32, (18, width), 1)
        entry = lax.broadcasted_iota(jnp.int32, (18, width), 0)
        block = sum((lane >= 96 * n).astype(jnp.int32) for n in range(1, len(blocks)))
        channel = (lane - 96 * block) >> 4
        part = (channel >= 3).astype(jnp.int32)
        at = lax.broadcasted_iota(jnp.int32, (256, width), 1)
        gap = (at & 15) - (lax.broadcasted_iota(jnp.int32, (256, width), 0) & 7)
        total = jnp.zeros((256, width), F32)
        for a in range(3):
            table = (entry == part * 6 + a * 3 + channel).astype(F32)
            picked = None
            for n in sorted({frame for frame, _ in blocks}):
                mine = sum(
                    jnp.where(block == k, table, 0.0)
                    for k, (frame, _) in enumerate(blocks)
                    if frame == n
                )
                term = dot_exact(joint[n], mine)
                picked = term if picked is None else picked + term
            wide = jnp.broadcast_to(picked[:, None, :], (32, 8, width)).reshape(256, width)
            total = jnp.where(gap == a, wide, total)
        high = total.astype(BF16).astype(F32)
        for k, (_, rest) in enumerate(blocks):
            if rest:
                inside = (at >= 96 * k) & (at < 96 * k + 96)
                high = jnp.where(inside, total - high, high)
        return high.astype(BF16)

    near = build(((0, False), (0, True), (1, False), (1, False), (1, True)))
    far = build(((2, False), (2, True)))
    return near, far


def near_kernel(
    core_ref, own_ref, x_ref, mask_ref, temporal_ref, spatial_ref, maps_ref,
    acc_ref, far_ref, out_ref, lay, m_ref,
):
    m_ref[...], far_ref[...] = mixing_matrices(temporal_ref, spatial_ref)
    own = own_ref[...] - 0.5 * lost_part(x_ref[...], mask_ref[...], maps_ref)
    out_ref[...] = own
    spread(lay, [core_ref[...].astype(F32), own])
    for i in range(SIDE // 8):
        near = lay[0:6, 8 * i : 8 * i + 16, :].reshape(6 * 16, SIDE).astype(BF16)
        window = lay[6:12, 8 * i : 8 * i + 16, :].reshape(6 * 16, SIDE)
        high = window.astype(BF16)
        low = (window - high.astype(F32)).astype(BF16)
        acc_ref[i] = dot_nn(m_ref[...], jnp.concatenate([near, near, high, low, high], 0))


def refine_kernel(chip_ref, own_ref, acc_ref, m_ref, p_ref, out_hbm, lay, out_ref, sems):
    spread(lay, [chip_ref[...].astype(F32)])
    steps = SIDE // 8
    copies = []
    for i in range(steps):
        window = lay[:, 8 * i : 8 * i + 16, :].reshape(6 * 16, SIDE).astype(BF16)
        mix = dot_nn(m_ref[...], jnp.concatenate([window, window], 0)) + acc_ref[i]
        re = None
        im = None
        for o in range(32):
            v = jnp.maximum(mix[8 * o : 8 * o + 8], 0.0)
            re = v * p_ref[0, o] if re is None else re + v * p_ref[0, o]
            im = v * p_ref[1, o] if im is None else im + v * p_ref[1, o]
        rows = slice(8 * i, 8 * i + 8)
        out_ref[rows, :] = own_ref[rows, :] + jnp.concatenate([re, im], 1)
        if i % 6 == 5:
            part = pl.ds(8 * (i - 5), 48)
            copies.append(
                pltpu.make_async_copy(out_ref.at[part], out_hbm.at[part], sems.at[i // 6])
            )
            copies[-1].start()
    for copy in copies:
        copy.wait()


def params(mib):
    return pltpu.CompilerParams(vmem_limit_bytes=mib * 1024 * 1024)


def groups(cuts, frames):
    found = {}
    for c in range(cuts):
        for f in range(frames):
            found.setdefault((c % (cuts // MB), f // G), []).append(c * frames + f)
    return list(found.values())


def cost(flops, moved):
    return pl.CostEstimate(flops=flops, bytes_accessed=moved, transcendentals=0)


def on_device(
    cine_image,
    coil_maps,
    caipi_shift,
    line_mask,
    measured,
    spatial_weight,
    temporal_weight,
    project_weight,
):
    cuts = lax.axis_size("cuts")
    frames = lax.axis_size("frame")
    image = cine_image[0, 0]
    send = pl.pallas_call(
        pack_kernel,
        out_shape=jax.ShapeDtypeStruct((PEERS, CHUNK, 2 * SIDE), BF16),
        in_specs=[HBM, HBM, HBM, HBM, HBM, HBM],
        out_specs=HBM,
        scratch_shapes=[
            pltpu.SMEM((1,), jnp.int32),
            pltpu.VMEM((SIDE, 2 * SIDE), F32),
            pltpu.VMEM((PER, SIDE, 2 * SIDE), BF16),
            pltpu.VMEM((COILS, QR, 2 * SIDE), BF16),
            pltpu.VMEM((1, SIDE), jnp.int32),
            pltpu.VMEM((4 * SIDE, 2 * SIDE), BF16),
            pltpu.VMEM((8, SIDE, 2 * SIDE), F32),
            pltpu.VMEM((PEERS, CHUNK, 2 * SIDE), BF16),
            pltpu.SemaphoreType.DMA((6,)),
            pltpu.SemaphoreType.DMA((PEERS,)),
        ],
        compiler_params=params(58),
        name="pack",
    )(
        caipi_shift,
        image,
        coil_maps[0],
        measured[0, 0],
        line_mask,
        jnp.asarray(width_matrix()),
    )
    where = groups(cuts, frames)
    got = lax.all_to_all(send, ("cuts", "frame"), 0, 0, axis_index_groups=where)
    slab = pl.pallas_call(
        slab_kernel,
        out_shape=jax.ShapeDtypeStruct((PEERS, 2 * SLAB, 2 * SIDE), BF16),
        in_specs=[VMEM, VMEM],
        out_specs=VMEM,
        scratch_shapes=[
            pltpu.VMEM((PEERS, 2, 8, 512), F32),
            pltpu.VMEM((PEERS, 5, 8, 512), F32),
            pltpu.VMEM((MB, 40 * G, 2 * SIDE), F32),
            pltpu.VMEM((MB, 40 * G, 512), F32),
        ],
        compiler_params=params(32),
        name="slab",
    )(got, jnp.asarray(slab_matrices()))
    back = lax.all_to_all(slab, ("cuts", "frame"), 0, 0, axis_index_groups=where)
    updated, edge = pl.pallas_call(
        update_kernel,
        out_shape=(
            jax.ShapeDtypeStruct((SIDE, 2 * SIDE), F32),
            jax.ShapeDtypeStruct((SIDE, 2 * SIDE), BF16),
        ),
        in_specs=[SMEM, VMEM, VMEM],
        out_specs=(VMEM, VMEM),
        scratch_shapes=[pltpu.VMEM((SIDE, 2 * SIDE), F32), pltpu.VMEM((SIDE, 2 * SIDE), F32)],
        compiler_params=params(16),
        name="update",
    )(caipi_shift, image, back)
    on_chip = lax.ppermute(edge, "frame", [(i, i ^ 1) for i in range(frames)])
    off_chip = lax.ppermute(
        edge, "frame", [(i, (i + 1) % frames if i % 2 else (i - 1) % frames) for i in range(frames)]
    )
    mixed, far_matrix, own = pl.pallas_call(
        near_kernel,
        out_shape=(
            jax.ShapeDtypeStruct((SIDE // 8, 256, SIDE), F32),
            jax.ShapeDtypeStruct((256, 192), BF16),
            jax.ShapeDtypeStruct((SIDE, 2 * SIDE), F32),
        ),
        in_specs=[VMEM, VMEM, VMEM, VMEM, VMEM, VMEM, VMEM],
        out_specs=(VMEM, VMEM, VMEM),
        scratch_shapes=[
            pltpu.VMEM((12, 208, SIDE), F32),
            pltpu.VMEM((256, 480), BF16),
        ],
        compiler_params=params(24),
        cost_estimate=cost(24 * 2 * 256 * 480 * 192, 6 * 2**20),
        name="near",
    )(
        on_chip,
        updated,
        image,
        line_mask,
        temporal_weight,
        spatial_weight.reshape(32, 18),
        coil_maps[0],
    )
    refined = pl.pallas_call(
        refine_kernel,
        out_shape=jax.ShapeDtypeStruct((SIDE, 2 * SIDE), F32),
        in_specs=[VMEM, VMEM, VMEM, VMEM, SMEM],
        out_specs=HBM,
        scratch_shapes=[
            pltpu.VMEM((6, 208, SIDE), F32),
            pltpu.VMEM((SIDE, 2 * SIDE), F32),
            pltpu.SemaphoreType.DMA((4,)),
        ],
        compiler_params=params(24),
        name="refine",
    )(off_chip, own, mixed, far_matrix, project_weight)
    return refined[None, None]


def solution(mesh):
    return jax.shard_map(
        on_device,
        mesh=mesh,
        in_specs=(
            P("cuts", "frame", None, None),
            P("cuts", None, None, None),
            P("cuts"),
            P("frame", None),
            P("cuts", "frame", None, None, None),
            P(),
            P(),
            P(),
        ),
        out_specs=P("cuts", "frame", None, None),
        check_vma=False,
    )
```
